256 devices in a mesh: dp: 32 (over x, z_lo, core), cent: 8 (over z_hi, y).
Axes of the slice: x: 4, y: 4, z: 8 (z_hi: 2, z_lo: 4; z = z_hi * 4 + z_lo), core: 2. Of those that a mesh axis runs over, the one named last changes fastest.
Arguments:
- embeddings: float32 [65536, 1024], P('dp'), may hold values from -100 to 100, as said below
- centroids: float32 [4096, 1024], P('cent'), may hold values from -5 to 5
- coarse_centroids: float32 [512, 1024], replicated, may hold values from -5 to 5
- top_centroids: float32 [64, 1024], replicated, may hold values from -5 to 5
Outputs:
- new_fine: float32 [8, 512, 1024], P('cent', 'dp')
- new_coarse: float32 [512, 1024], replicated
- new_top: float32 [64, 1024], replicated
The draws below stay inside these ranges and needn't reach their ends.
Inputs may be any that keep to these rules, and one draw needn't show every extreme that they name: `embeddings`: embeddings are real-valued feature vectors.
All inputs are finite; a program needn't handle non-finite values.
Results may differ from the reference program's by a relative error of at most 0.0003.
Values sent between devices are 32-bit elements; how exact they have to be, the bound alone decides.
No kernel may reach another device: no remote copies, remote signals or barrier semaphores. Data moves between devices by JAX's collectives and lax.ppermute only.
A program may use at most 64 MiB of HBM per device.

```python
import jax
import jax.numpy as jnp
from jax import lax

D = 1024
K1 = 4096
K2 = 512
K3 = 64
ROWS_DEV = 2048
ROWS = 65536
N_DP = 32
N_CENT = 8


def base_centers(source):
    return jax.random.truncated_normal(source, -4.0, 4.0, (K1, D), jnp.float32)


def draw_centroids(key, part):
    base_rows = base_centers(key)
    return base_rows


def draw_embeddings(key, part):
    seeded = jax.random.fold_in(key, 7)
    first_key = jax.random.fold_in(seeded, 0)
    values = jax.random.truncated_normal(first_key, -4.0, 4.0, (ROWS, D), jnp.float32)
    return values


def scatter_about(key, dims, scale, bound, held_as=jnp.bfloat16):
    drawn = jax.random.normal(key, dims, jnp.float32) * scale
    return jnp.minimum(jnp.maximum(drawn, -bound), bound).astype(held_as)


def setup_inputs(seed: int = 0) -> dict:
    seeds = jax.random.split(jax.random.key(seed), 5)
    embeddings = draw_embeddings(jax.random.fold_in(seeds[4], 71), 0)
    centroids = draw_centroids(jax.random.fold_in(seeds[4], 71), 0)
    coarse_centroids = scatter_about(seeds[2], (K2, D), 1.0, 5.0, jnp.float32)
    top_centroids = scatter_about(seeds[3], (K3, D), 1.0, 5.0, jnp.float32)
    return {"embeddings": embeddings, "centroids": centroids, "coarse_centroids": coarse_centroids, "top_centroids": top_centroids}


epsilon = 1e-06
SHARPNESS = 1.5

def unit_rms(points):
    return points * lax.rsqrt(lax.optimization_barrier(jnp.mean(points * points, axis=1, keepdims=True)) + epsilon)

def soft_fit(points, centers):
    inv_norm = lax.rsqrt(lax.optimization_barrier(jnp.sum(centers * centers, axis=1)) + epsilon)
    logits = SHARPNESS * jnp.dot(points, centers.T, precision=lax.Precision.HIGHEST, preferred_element_type=jnp.float32) * inv_norm[None, :]
    row_top = lax.optimization_barrier(jnp.max(logits, axis=1))
    shifted = jnp.exp(logits - row_top[:, None])
    row_total = lax.optimization_barrier(jnp.sum(shifted, axis=1))
    weights = shifted / row_total[:, None]
    numerator = jnp.dot(weights.T, points, precision=lax.Precision.HIGHEST, preferred_element_type=jnp.float32)
    return (numerator, lax.optimization_barrier(jnp.sum(weights, axis=0)))

def reference(embeddings, centroids, coarse_centroids, top_centroids):
    blocks = embeddings.reshape(N_DP, ROWS_DEV, D)
    start = (jnp.zeros((K1, D), jnp.float32), jnp.zeros((K1,), jnp.float32))

    def accumulate(carry, block):
        numerator, col_mass = soft_fit(block, centroids)
        return ((carry[0] + numerator, carry[1] + col_mass), None)
    (fine_sums, fine_mass), _ = lax.scan(accumulate, start, blocks)
    fine_flat = fine_sums / fine_mass[:, None]
    coarse_sums, coarse_mass = soft_fit(unit_rms(fine_flat), coarse_centroids)
    new_coarse = coarse_sums / coarse_mass[:, None]
    top_sums, top_mass = soft_fit(unit_rms(new_coarse), top_centroids)
    new_top = top_sums / top_mass[:, None]
    return (fine_flat.reshape(N_CENT, K1 // N_CENT, D), new_coarse, new_top)
```

```python
import jax
import jax.numpy as jnp
from jax import lax
from jax.sharding import Mesh, PartitionSpec as P

epsilon = 1e-06
SHARPNESS = 1.5
DP = ("x", "zl", "c")
CENT = ("zh", "y")
RING = ("zl", "zh", "y")
MASS = 128


def dot3(left, right, contract_left, contract_right):
    return lax.dot_general(
        left,
        right,
        (((contract_left,), (contract_right,)), ((), ())),
        precision=lax.Precision.HIGH,
        preferred_element_type=jnp.float32,
    )


def unit_rms(points):
    return points * lax.rsqrt(jnp.mean(points * points, axis=1, keepdims=True) + epsilon)


def center_logits(points, centers):
    inv_norm = lax.rsqrt(jnp.sum(centers * centers, axis=1) + epsilon)
    return SHARPNESS * dot3(points, centers, 1, 1) * inv_norm[None, :]


def softmax(logits):
    shifted = jnp.exp(logits - jnp.max(logits, axis=1, keepdims=True))
    return shifted / jnp.sum(shifted, axis=1, keepdims=True)


def spread(value, axes, size):
    return lax.all_to_all(jnp.broadcast_to(value[None], (size, *value.shape)), axes, 0, 0)


def with_mass(sums, mass):
    return jnp.concatenate([sums, jnp.broadcast_to(mass[:, None], (mass.shape[0], MASS))], axis=1)


def swap_core(value):
    return lax.ppermute(value, "c", [(0, 1), (1, 0)])


def body(embeddings, centroids, coarse_centroids, top_centroids):
    core = lax.axis_index("c")
    x = lax.axis_index("x")
    dim = embeddings.shape[1]
    centroids = centroids.reshape(4, 4, 2, 16, dim).transpose(2, 0, 1, 3, 4).reshape(512, dim)

    logits = center_logits(embeddings, centroids)
    own_top = jnp.max(logits, axis=1)
    shifted = jnp.exp(logits - own_top[:, None])
    own_total = jnp.sum(shifted, axis=1)
    stats = spread(jnp.stack([own_top, own_total]), CENT, 8)
    row_top = jnp.max(stats[:, 0], axis=0)
    row_total = jnp.sum(stats[:, 1] * jnp.exp(stats[:, 0] - row_top[None]), axis=0)
    weights = shifted * (jnp.exp(own_top - row_top) / row_total)[:, None]

    part = with_mass(dot3(weights, embeddings, 0, 0), jnp.sum(weights, axis=0))
    keep = lax.dynamic_slice_in_dim(part, core * 256, 256, 0)
    give = lax.dynamic_slice_in_dim(part, (1 - core) * 256, 256, 0)
    part = keep + swap_core(give)
    part = jnp.sum(lax.all_to_all(part.reshape(4, 64, dim + MASS), "x", 0, 0), axis=0)
    part = jnp.sum(lax.all_to_all(part.reshape(4, 16, dim + MASS), "zl", 0, 0), axis=0)
    fine = part[:, :dim] / part[:, dim : dim + 1]

    points = spread(unit_rms(fine), "x", 4).reshape(64, dim)
    points = jnp.concatenate([points, swap_core(points)], axis=0)
    weights = softmax(center_logits(points, coarse_centroids))
    weights = lax.dynamic_slice_in_dim(weights, (core * 4 + x) * 64, 64, 1)
    part = with_mass(dot3(weights, points, 0, 0), jnp.sum(weights, axis=0))
    part = jnp.sum(lax.all_to_all(part.reshape(32, 2, dim + MASS), RING, 0, 0), axis=0)
    coarse = part[:, :dim] / part[:, dim : dim + 1]
    coarse = spread(coarse, RING, 32).reshape(64, dim)
    coarse = spread(coarse, "x", 4).reshape(256, dim)
    other = swap_core(coarse)
    new_coarse = jnp.concatenate(
        [jnp.where(core == 0, coarse, other), jnp.where(core == 0, other, coarse)], axis=0
    )

    points = unit_rms(new_coarse)
    weights = softmax(center_logits(points, top_centroids))
    new_top = dot3(weights, points, 0, 0) / jnp.sum(weights, axis=0)[:, None]
    return (fine[None], new_coarse, new_top)


def solution(mesh):
    fold = Mesh(mesh.devices.reshape(4, 4, 2, 2, 4), DP + CENT)
    in_specs = (P(DP, None), P(CENT, None), P(), P())
    out_specs = (P(CENT, DP, None), P(), P())
    return jax.shard_map(body, mesh=fold, in_specs=in_specs, out_specs=out_specs, check_vma=False)
```

```python
import functools

import jax
import jax.numpy as jnp
from jax import lax
from jax.experimental import pallas as pl
from jax.experimental.pallas import tpu as pltpu
from jax.sharding import Mesh, PartitionSpec as P

epsilon = 1e-06
SHARPNESS = 1.5
DP = ("x", "zl", "c")
CENT = ("zh", "y")
MASS = 128
F32, BF16 = jnp.float32, jnp.bfloat16
VMEM = 24 * 2**20
NT = (((1,), (1,)), ((), ()))
NN = (((1,), (0,)), ((), ()))


def split(value):
    high = value.astype(BF16)
    return high, (value - high.astype(F32)).astype(BF16)


def mm(left, right, dims):
    return lax.dot_general(left, right, dims, preferred_element_type=F32)


def fit_kernel(step, e_ref, c_ref, p_ref, stat_ref, eh_ref, el_ref, ch, cl):
    @pl.when(pl.program_id(0) == 0)
    def _():
        c = c_ref[...]
        c = c * (SHARPNESS * lax.rsqrt(jnp.sum(c * c, axis=1, keepdims=True) + epsilon))
        high, low = split(c)
        for chip in range(16):
            for core in range(2):
                here, there = (chip * 2 + core) * 16, (core * 16 + chip) * 16
                ch[there : there + 16, :] = high[here : here + 16, :]
                cl[there : there + 16, :] = low[here : here + 16, :]

    for j in range(0, e_ref.shape[0], step):
        rows = slice(j, j + step)
        eh, el = split(e_ref[rows, :])
        eh_ref[rows, :] = eh
        el_ref[rows, :] = el
        logits = mm(ch[...], eh, NT) + mm(ch[...], el, NT) + mm(cl[...], eh, NT)
        top = jnp.max(logits, axis=0, keepdims=True)
        p = jnp.exp(logits - top)
        p_ref[:, rows] = p
        stat_ref[0:1, rows] = top
        stat_ref[1:2, rows] = jnp.sum(p, axis=0, keepdims=True)


def fit(e, c, block=512, step=256):
    (n, d), k = e.shape, c.shape[0]
    return pl.pallas_call(
        functools.partial(fit_kernel, step),
        grid=(n // block,),
        in_specs=[pl.BlockSpec((block, d), lambda i: (i, 0)), pl.BlockSpec((k, d), lambda i: (0, 0))],
        out_specs=[
            pl.BlockSpec((k, block), lambda i: (0, i)),
            pl.BlockSpec((2, block), lambda i: (0, i)),
            pl.BlockSpec((block, d), lambda i: (i, 0)),
            pl.BlockSpec((block, d), lambda i: (i, 0)),
        ],
        out_shape=[
            jax.ShapeDtypeStruct((k, n), F32),
            jax.ShapeDtypeStruct((2, n), F32),
            jax.ShapeDtypeStruct((n, d), BF16),
            jax.ShapeDtypeStruct((n, d), BF16),
        ],
        scratch_shapes=[pltpu.VMEM((k, d), BF16)] * 2,
        compiler_params=pltpu.CompilerParams(vmem_limit_bytes=VMEM),
        name="fit",
    )(e, c)


def sums_kernel(_, stats_ref, own_ref, p_ref, eh_ref, el_ref, o_ref):
    @pl.when(pl.program_id(0) == 0)
    def _():
        o_ref[...] = jnp.zeros_like(o_ref)

    tops, totals = stats_ref[:, 0, :], stats_ref[:, 1, :]
    top = jnp.max(tops, axis=0, keepdims=True)
    total = jnp.sum(totals * jnp.exp(tops - top), axis=0, keepdims=True)
    w = p_ref[...] * (jnp.exp(own_ref[0:1, :] - top) / total)
    wh, wl = split(w)
    d = eh_ref.shape[1]
    o_ref[:, d:] += jnp.broadcast_to(jnp.sum(w, axis=1, keepdims=True), (w.shape[0], MASS))
    o_ref[:, :d] += mm(wh, eh_ref[...], NN) + mm(wh, el_ref[...], NN) + mm(wl, eh_ref[...], NN)


def sums(stats, own, p, eh, el, half, block=1024):
    n, d = eh.shape
    k = p.shape[0] // 2
    return pl.pallas_call(
        sums_kernel,
        grid_spec=pltpu.PrefetchScalarGridSpec(
            num_scalar_prefetch=1,
            grid=(n // block,),
            in_specs=[
                pl.BlockSpec((8, 2, block), lambda i, half: (0, 0, i)),
                pl.BlockSpec((2, block), lambda i, half: (0, i)),
                pl.BlockSpec((k, block), lambda i, half: (half[0], i)),
                pl.BlockSpec((block, d), lambda i, half: (i, 0)),
                pl.BlockSpec((block, d), lambda i, half: (i, 0)),
            ],
            out_specs=pl.BlockSpec((k, d + MASS), lambda i, half: (0, 0)),
        ),
        out_shape=jax.ShapeDtypeStruct((k, d + MASS), F32),
        compiler_params=pltpu.CompilerParams(vmem_limit_bytes=VMEM),
        cost_estimate=pl.CostEstimate(flops=6 * n * d * k, bytes_accessed=12 * n * k, transcendentals=0),
        name="sums",
    )(half, stats, own, p, eh, el)


def dot3(left, right, contract_left, contract_right):
    return lax.dot_general(
        left,
        right,
        (((contract_left,), (contract_right,)), ((), ())),
        precision=lax.Precision.HIGH,
        preferred_element_type=F32,
    )


def unit_rms(points):
    return points * lax.rsqrt(jnp.mean(points * points, axis=1, keepdims=True) + epsilon)


def center_logits(points, centers):
    inv_norm = lax.rsqrt(jnp.sum(centers * centers, axis=1) + epsilon)
    return SHARPNESS * dot3(points, centers, 1, 1) * inv_norm[None, :]


def softmax(logits):
    shifted = jnp.exp(logits - jnp.max(logits, axis=1, keepdims=True))
    return shifted / jnp.sum(shifted, axis=1, keepdims=True)


def spread(value, axes, size):
    return lax.all_to_all(jnp.broadcast_to(value[None], (size, *value.shape)), axes, 0, 0)


def add_up(part, axes, size):
    part = part.reshape(size, part.shape[0] // size, part.shape[1])
    return jnp.sum(lax.all_to_all(part, axes, 0, 0), axis=0)


def with_mass(sums, mass):
    return jnp.concatenate([sums, jnp.broadcast_to(mass[:, None], (mass.shape[0], MASS))], axis=1)


def swap_core(value):
    return lax.ppermute(value, "c", [(0, 1), (1, 0)])


def body(embeddings, centroids, coarse_centroids, top_centroids):
    core = lax.axis_index("c")
    dim = embeddings.shape[1]
    embeddings, centroids = (pltpu.with_memory_space_constraint(a, pltpu.HBM) for a in (embeddings, centroids))
    p, own, eh, el = fit(embeddings, centroids)
    mine, theirs = core.reshape(1), 1 - core.reshape(1)
    own, mine, theirs = lax.optimization_barrier((own, mine, theirs))
    stats = spread(own, CENT, 8)
    part = swap_core(sums(stats, own, p, eh, el, theirs)) + sums(stats, own, p, eh, el, mine)
    part = add_up(add_up(part, "x", 4), "zl", 4)
    fine = part[:, :dim] / part[:, dim : dim + 1]

    points = spread(unit_rms(fine), "x", 4).reshape(64, dim)
    points = jnp.concatenate([points, swap_core(points)], axis=0)
    weights = softmax(center_logits(points, coarse_centroids))
    weights = lax.dynamic_slice_in_dim(weights, (core * 4 + lax.axis_index("x")) * 64, 64, 1)
    part = with_mass(dot3(weights, points, 0, 0), jnp.sum(weights, axis=0))
    part = add_up(part, ("y", "zh", "zl"), 32)
    coarse = part[:, :dim] / part[:, dim : dim + 1]
    coarse = spread(coarse, ("zh", "zl"), 8).reshape(16, dim)
    coarse = spread(coarse, ("x", "y"), 16).reshape(256, dim)
    other = swap_core(coarse)
    new_coarse = jnp.concatenate(
        [jnp.where(core == 0, coarse, other), jnp.where(core == 0, other, coarse)], axis=0
    )

    points = unit_rms(new_coarse)
    weights = softmax(center_logits(points, top_centroids))
    new_top = dot3(weights, points, 0, 0) / jnp.sum(weights, axis=0)[:, None]
    return (fine[None], new_coarse, new_top)


def solution(mesh):
    fold = Mesh(mesh.devices.reshape(4, 4, 2, 2, 4), DP + CENT)
    in_specs = (P(DP, None), P(CENT, None), P(), P())
    out_specs = (P(CENT, DP, None), P(), P())
    return jax.shard_map(body, mesh=fold, in_specs=in_specs, out_specs=out_specs, check_vma=False)
```

```python
import functools

import jax
import jax.numpy as jnp
from jax import lax
from jax.experimental import pallas as pl
from jax.experimental.pallas import tpu as pltpu
from jax.sharding import Mesh, PartitionSpec as P

epsilon = 1e-06
SHARPNESS = 1.5
DP = ("x", "zl", "c")
CENT = ("zh", "y")
MASS = 128
F32, BF16 = jnp.float32, jnp.bfloat16
VMEM = 24 * 2**20
NT = (((1,), (1,)), ((), ()))
NN = (((1,), (0,)), ((), ()))


def split(value):
    high = value.astype(BF16)
    return high, (value - high.astype(F32)).astype(BF16)


def mm(left, right, dims):
    return lax.dot_general(left, right, dims, preferred_element_type=F32)


def fit_kernel(step, e_ref, c_ref, p_ref, stat_ref, eh_ref, el_ref, chl):
    @pl.when(pl.program_id(0) == 0)
    def _():
        c = c_ref[...]
        c = c * (SHARPNESS * lax.rsqrt(jnp.sum(c * c, axis=1, keepdims=True) + epsilon))
        high, low = split(c)
        for chip in range(16):
            for core in range(2):
                here, there = (chip * 2 + core) * 16, (core * 16 + chip) * 16
                chl[there : there + 16, :] = high[here : here + 16, :]
                chl[512 + there : 528 + there, :] = low[here : here + 16, :]

    for j in range(0, e_ref.shape[0], step):
        rows = slice(j, j + step)
        eh, el = split(e_ref[rows, :])
        eh_ref[rows, :] = eh
        el_ref[rows, :] = el
        k = p_ref.shape[0]
        both = mm(chl[...], eh, NT)
        logits = both[:k] + both[k:] + mm(chl[:k, :], el, NT)
        top = jnp.max(logits, axis=0, keepdims=True)
        p = jnp.exp(logits - top)
        p_ref[:, rows] = p
        stat_ref[0:1, rows] = top
        stat_ref[1:2, rows] = jnp.sum(p, axis=0, keepdims=True)


def fit(e, c, block=512, step=256):
    (n, d), k = e.shape, c.shape[0]
    return pl.pallas_call(
        functools.partial(fit_kernel, step),
        grid=(n // block,),
        in_specs=[pl.BlockSpec((block, d), lambda i: (i, 0)), pl.BlockSpec((k, d), lambda i: (0, 0))],
        out_specs=[
            pl.BlockSpec((k, block), lambda i: (0, i)),
            pl.BlockSpec((2, block), lambda i: (0, i)),
            pl.BlockSpec((block, d), lambda i: (i, 0)),
            pl.BlockSpec((block, d), lambda i: (i, 0)),
        ],
        out_shape=[
            jax.ShapeDtypeStruct((k, n), F32),
            jax.ShapeDtypeStruct((2, n), F32),
            jax.ShapeDtypeStruct((n, d), BF16),
            jax.ShapeDtypeStruct((n, d), BF16),
        ],
        scratch_shapes=[pltpu.VMEM((2 * k, d), BF16)],
        compiler_params=pltpu.CompilerParams(vmem_limit_bytes=VMEM),
        name="fit",
    )(e, c)


def sums_kernel(_, stats_ref, own_ref, eh_ref, el_ref, *refs):
    *p_refs, o_ref = refs

    @pl.when(pl.program_id(0) == 0)
    def _():
        o_ref[...] = jnp.zeros_like(o_ref)

    tops, totals = stats_ref[:, 0, :], stats_ref[:, 1, :]
    top = jnp.max(tops, axis=0, keepdims=True)
    total = jnp.sum(totals * jnp.exp(tops - top), axis=0, keepdims=True)
    scale = jnp.exp(own_ref[0:1, :] - top) / total
    w = jnp.concatenate([p_ref[...] for p_ref in p_refs], axis=0) * scale
    (k, block), d = w.shape, eh_ref.shape[1]
    here = pl.ds(pl.multiple_of(pl.program_id(0) * block, block), block)
    wh, wl = split(w)
    both = mm(jnp.concatenate([wh, wl], axis=0), eh_ref[here, :], NN)
    part = both[:k] + both[k:] + mm(wh, el_ref[here, :], NN)
    mass = jnp.broadcast_to(jnp.sum(w, axis=1, keepdims=True), (k, MASS))
    o_ref[:, :d] += part
    o_ref[:, d:] += mass


def sums(stats, own, p, eh, el, blocks, rows=64, block=1024):
    n, d = eh.shape
    count = blocks.shape[0]
    whole = pl.BlockSpec(memory_space=pltpu.VMEM)
    return pl.pallas_call(
        sums_kernel,
        grid_spec=pltpu.PrefetchScalarGridSpec(
            num_scalar_prefetch=1,
            grid=(n // block,),
            in_specs=[
                pl.BlockSpec((8, 2, block), lambda i, b: (0, 0, i)),
                pl.BlockSpec((2, block), lambda i, b: (0, i)),
                whole,
                whole,
            ]
            + [pl.BlockSpec((rows, block), lambda i, b, j=j: (b[j], i)) for j in range(count)],
            out_specs=pl.BlockSpec((rows * count, d + MASS), lambda i, b: (0, 0)),
        ),
        out_shape=jax.ShapeDtypeStruct((rows * count, d + MASS), F32),
        compiler_params=pltpu.CompilerParams(vmem_limit_bytes=VMEM),
        cost_estimate=pl.CostEstimate(flops=6 * n * d * rows * count, bytes_accessed=4 * n * d, transcendentals=0),
        name="sums",
    )(blocks, stats, own, eh, el, *[p] * count)


def prepare_kernel(c_ref, o_ref):
    c = c_ref[...]
    k = c.shape[0]
    o_ref[:k, :], o_ref[k:, :] = split(c * (SHARPNESS * lax.rsqrt(jnp.sum(c * c, axis=1, keepdims=True) + epsilon)))


def prepare(c):
    return pl.pallas_call(
        prepare_kernel,
        out_shape=jax.ShapeDtypeStruct((2 * c.shape[0], c.shape[1]), BF16),
        compiler_params=pltpu.CompilerParams(vmem_limit_bytes=VMEM),
        name="prepare",
    )(c)


def unit_rms(points):
    return points * lax.rsqrt(jnp.mean(points * points, axis=1, keepdims=True) + epsilon)


def soft_weights(high, low, centers):
    k = centers.shape[0] // 2
    logits = mm(high, centers[:k, :], NT) + mm(high, centers[k:, :], NT) + mm(low, centers[:k, :], NT)
    shifted = jnp.exp(logits - jnp.max(logits, axis=1, keepdims=True))
    return (shifted / jnp.sum(shifted, axis=1, keepdims=True)).T


def store_sums(o_ref, w, high, low):
    wh, wl = split(w)
    d = high.shape[1]
    o_ref[:, :d] = mm(wh, high, NN) + mm(wh, low, NN) + mm(wl, high, NN)
    o_ref[:, d:] = jnp.broadcast_to(jnp.sum(w, axis=1, keepdims=True), (w.shape[0], MASS))


def points_kernel(part_ref, fine_ref, spread_ref):
    part = part_ref[0] + part_ref[1] + part_ref[2] + part_ref[3]
    d = fine_ref.shape[1]
    fine = part[:, :d] / part[:, d : d + 1]
    fine_ref[...] = fine
    points = unit_rms(fine)
    for i in range(spread_ref.shape[0]):
        spread_ref[i] = points


def points_of(part, copies):
    _, n, d = part.shape
    return pl.pallas_call(
        points_kernel,
        out_shape=[
            jax.ShapeDtypeStruct((n, d - MASS), F32),
            jax.ShapeDtypeStruct((copies, n, d - MASS), F32),
        ],
        compiler_params=pltpu.CompilerParams(vmem_limit_bytes=VMEM),
        name="points",
    )(part)


def coarse_kernel(slice_ref, own_ref, other_ref, c_ref, o_ref, w_ref):
    high, low = split(jnp.concatenate([own_ref[...], other_ref[...]], axis=0))
    w_ref[...] = soft_weights(high, low, c_ref[...])
    rows = o_ref.shape[0]
    w = w_ref[pl.ds(pl.multiple_of(slice_ref[0] * rows, rows), rows), :]
    store_sums(o_ref, w, high, low)


def coarse_sums(index, own, other, centers, rows):
    n, d = own.shape
    whole = pl.BlockSpec(memory_space=pltpu.VMEM)
    return pl.pallas_call(
        coarse_kernel,
        in_specs=[pl.BlockSpec(memory_space=pltpu.SMEM), whole, whole, whole],
        out_specs=whole,
        out_shape=jax.ShapeDtypeStruct((rows, d + MASS), F32),
        scratch_shapes=[pltpu.VMEM((centers.shape[0] // 2, 2 * n), F32)],
        compiler_params=pltpu.CompilerParams(vmem_limit_bytes=VMEM),
        name="coarse",
    )(index, own, other, centers)


def top_kernel(points_ref, c_ref, o_ref):
    high, low = split(unit_rms(points_ref[...]))
    store_sums(o_ref, soft_weights(high, low, c_ref[...]), high, low)


def top_sums(points, centers):
    d = points.shape[1]
    whole = pl.BlockSpec(memory_space=pltpu.VMEM)
    return pl.pallas_call(
        top_kernel,
        in_specs=[whole, whole],
        out_specs=whole,
        out_shape=jax.ShapeDtypeStruct((centers.shape[0] // 2, d + MASS), F32),
        compiler_params=pltpu.CompilerParams(vmem_limit_bytes=VMEM),
        name="top",
    )(points, centers)


def final_kernel(core_ref, own_ref, other_ref, part_ref, add_ref, coarse_ref, top_ref, sems):
    rows = own_ref.shape[0]
    copies = []
    for i, ref in enumerate((own_ref, other_ref)):
        half = core_ref[0] if i == 0 else 1 - core_ref[0]
        there = pl.ds(pl.multiple_of(half * rows, rows), rows)
        copies.append(pltpu.make_async_copy(ref, coarse_ref.at[there, :], sems.at[i]))
        copies[i].start()
    part = part_ref[...] + add_ref[...]
    d = top_ref.shape[1]
    top_ref[...] = part[:, :d] / part[:, d : d + 1]
    for copy in copies:
        copy.wait()


def final(core, own, other, part, add):
    whole = pl.BlockSpec(memory_space=pltpu.VMEM)
    (n, d), k = own.shape, part.shape[0]
    return pl.pallas_call(
        final_kernel,
        in_specs=[pl.BlockSpec(memory_space=pltpu.SMEM)] + [whole] * 4,
        out_specs=[pl.BlockSpec(memory_space=pltpu.HBM), whole],
        out_shape=[jax.ShapeDtypeStruct((2 * n, d), F32), jax.ShapeDtypeStruct((k, d), F32)],
        scratch_shapes=[pltpu.SemaphoreType.DMA((2,))],
        compiler_params=pltpu.CompilerParams(vmem_limit_bytes=VMEM),
        name="final",
    )(core, own, other, part, add)


def spread(value, axes, size):
    return lax.all_to_all(jnp.broadcast_to(value[None], (size, *value.shape)), axes, 0, 0)


def add_up(part, axes, size):
    part = part.reshape(size, part.shape[0] // size, part.shape[1])
    return jnp.sum(lax.all_to_all(part, axes, 0, 0), axis=0)


def swap_core(value):
    return lax.ppermute(value, "c", [(0, 1), (1, 0)])


def shift(value, step):
    return lax.ppermute(value, "x", [(i, (i + step) % 4) for i in range(4)])


def body(embeddings, centroids, coarse_centroids, top_centroids):
    core = lax.axis_index("c")
    dim = embeddings.shape[1]
    embeddings, centroids = (pltpu.with_memory_space_constraint(a, pltpu.HBM) for a in (embeddings, centroids))
    p, own, eh, el = fit(embeddings, centroids)
    x = lax.axis_index("x")
    mine, theirs = 4 * core, 4 * (1 - core)
    up, down, far = (x + 1) % 4, (x + 3) % 4, (x + 2) % 4
    blocks = [
        jnp.stack(group)
        for group in (
            (theirs + far,),
            (mine + far,),
            (theirs + up, theirs + down, theirs + x),
            (mine + up, mine + down),
            (mine + x,),
        )
    ]
    own, blocks = lax.optimization_barrier((own, blocks))
    stats = spread(own, CENT, 8)
    far_in = swap_core(sums(stats, own, p, eh, el, blocks[0]))
    far_own = sums(stats, own, p, eh, el, blocks[1])
    near_in = swap_core(sums(stats, own, p, eh, el, blocks[2]))
    far_sum = far_own + far_in
    up_part, down_part = shift(far_sum[:32], 1), shift(far_sum[32:], -1)
    blocks[3], _ = lax.optimization_barrier((blocks[3], far_sum))
    near = sums(stats, own, p, eh, el, blocks[3]) + near_in[:128]
    up_sum = jnp.concatenate([near[:32] + up_part, near[32:64]], axis=0)
    down_sum = jnp.concatenate([near[64:96], near[96:] + down_part], axis=0)
    from_down, from_up = shift(up_sum, 1), shift(down_sum, -1)
    blocks[4], _ = lax.optimization_barrier((blocks[4], (up_sum, down_sum)))
    part = sums(stats, own, p, eh, el, blocks[4])
    part = part + near_in[128:] + from_down + from_up
    coarse_centroids, top_centroids, _ = lax.optimization_barrier((coarse_centroids, top_centroids, up_sum))
    coarse_centers, top_centers = prepare(coarse_centroids), prepare(top_centroids)
    fine, points = points_of(lax.all_to_all(part.reshape(4, 16, dim + MASS), "zl", 0, 0), 4)

    points = lax.all_to_all(points, "x", 0, 0).reshape(64, dim)
    part = coarse_sums((core * 4 + x).reshape(1), points, swap_core(points), coarse_centers, 64)
    part = add_up(part, ("y", "zh", "zl"), 32)
    coarse = part[:, :dim] / part[:, dim : dim + 1]
    coarse = spread(coarse, ("zh", "zl"), 8).reshape(16, dim)
    coarse = spread(coarse, ("x", "y"), 16).reshape(256, dim)
    other = swap_core(coarse)
    part = top_sums(coarse, top_centers)
    new_coarse, new_top = final(core.reshape(1), coarse, other, part, swap_core(part))
    return (fine[None], new_coarse, new_top)


def solution(mesh):
    fold = Mesh(mesh.devices.reshape(4, 4, 2, 2, 4), DP + CENT)
    in_specs = (P(DP, None), P(CENT, None), P(), P())
    out_specs = (P(CENT, DP, None), P(), P())
    return jax.shard_map(body, mesh=fold, in_specs=in_specs, out_specs=out_specs, check_vma=False)
```

```python
import functools

import jax
import jax.numpy as jnp
from jax import lax
from jax.experimental import pallas as pl
from jax.experimental.pallas import tpu as pltpu
from jax.sharding import Mesh, PartitionSpec as P

epsilon = 1e-06
SHARPNESS = 1.5
DP = ("x", "zl", "c")
CENT = ("zh", "y")
MASS = 128
F32, BF16 = jnp.float32, jnp.bfloat16
VMEM = 36 * 2**20
NT = (((1,), (1,)), ((), ()))
NN = (((1,), (0,)), ((), ()))


def split(value):
    high = value.astype(BF16)
    return high, (value - high.astype(F32)).astype(BF16)


def mm(left, right, dims):
    return lax.dot_general(left, right, dims, preferred_element_type=F32)


def fit_kernel(step, e_hbm, c_hbm, p_ref, stat_ref, eh_ref, el_ref, chl, c_ref, e_ref, sems):
    (n, _), k = e_ref.shape, c_ref.shape[0]
    pieces = 4
    copies = []
    for i in range(pieces):
        rows = pl.ds(i * (k // pieces), k // pieces)
        copies.append(pltpu.make_async_copy(c_hbm.at[rows, :], c_ref.at[rows, :], sems.at[n // step + i]))
    for i in range(n // step):
        rows = pl.ds(i * step, step)
        copies.append(pltpu.make_async_copy(e_hbm.at[rows, :], e_ref.at[rows, :], sems.at[i]))
    for copy in copies:
        copy.start()
    for chip in range(16):
        if chip % (16 // pieces) == 0:
            copies[chip // (16 // pieces)].wait()
        for core in range(2):
            here, there = (chip * 2 + core) * 16, (core * 16 + chip) * 16
            c = c_ref[here : here + 16, :]
            c = c * (SHARPNESS * lax.rsqrt(jnp.sum(c * c, axis=1, keepdims=True) + epsilon))
            chl[there : there + 16, :], chl[k + there : k + there + 16, :] = split(c)

    @pl.loop(0, n // step)
    def _(i):
        rows = pl.ds(pl.multiple_of(i * step, step), step)
        pltpu.make_async_copy(e_hbm.at[rows, :], e_ref.at[rows, :], sems.at[i]).wait()
        eh, el = split(e_ref[rows, :])
        eh_ref[rows, :] = eh
        el_ref[rows, :] = el
        both = mm(chl[...], eh, NT)
        logits = both[:k] + both[k:] + mm(chl[:k, :], el, NT)
        top = jnp.max(logits, axis=0, keepdims=True)
        p = jnp.exp(logits - top)
        p_ref[:, rows] = p
        stat_ref[0:1, rows] = top
        stat_ref[1:2, rows] = jnp.sum(p, axis=0, keepdims=True)


def fit(e, c, step=512):
    (n, d), k = e.shape, c.shape[0]
    return pl.pallas_call(
        functools.partial(fit_kernel, step),
        in_specs=[pl.BlockSpec(memory_space=pltpu.HBM)] * 2,
        out_specs=[pl.BlockSpec(memory_space=pltpu.VMEM)] * 4,
        out_shape=[
            jax.ShapeDtypeStruct((k, n), F32),
            jax.ShapeDtypeStruct((2, n), F32),
            jax.ShapeDtypeStruct((n, d), BF16),
            jax.ShapeDtypeStruct((n, d), BF16),
        ],
        scratch_shapes=[
            pltpu.VMEM((2 * k, d), BF16),
            pltpu.VMEM((k, d), F32),
            pltpu.VMEM((n, d), F32),
            pltpu.SemaphoreType.DMA((n // step + 4,)),
        ],
        compiler_params=pltpu.CompilerParams(vmem_limit_bytes=VMEM),
        name="fit",
    )(e, c)


def sums_kernel(_, stats_ref, own_ref, eh_ref, el_ref, *refs):
    *p_refs, o_ref = refs

    @pl.when(pl.program_id(0) == 0)
    def _():
        o_ref[...] = jnp.zeros_like(o_ref)

    tops, totals = stats_ref[:, 0, :], stats_ref[:, 1, :]
    top = jnp.max(tops, axis=0, keepdims=True)
    total = jnp.sum(totals * jnp.exp(tops - top), axis=0, keepdims=True)
    scale = jnp.exp(own_ref[0:1, :] - top) / total
    w = jnp.concatenate([p_ref[...] for p_ref in p_refs], axis=0) * scale
    (k, block), d = w.shape, eh_ref.shape[1]
    here = pl.ds(pl.multiple_of(pl.program_id(0) * block, block), block)
    wh, wl = split(w)
    both = mm(jnp.concatenate([wh, wl], axis=0), eh_ref[here, :], NN)
    part = both[:k] + both[k:] + mm(wh, el_ref[here, :], NN)
    mass = jnp.broadcast_to(jnp.sum(w, axis=1, keepdims=True), (k, MASS))
    o_ref[:, :d] += part
    o_ref[:, d:] += mass


def sums(stats, own, p, eh, el, blocks, rows=64, block=1024):
    n, d = eh.shape
    count = blocks.shape[0]
    whole = pl.BlockSpec(memory_space=pltpu.VMEM)
    return pl.pallas_call(
        sums_kernel,
        grid_spec=pltpu.PrefetchScalarGridSpec(
            num_scalar_prefetch=1,
            grid=(n // block,),
            in_specs=[
                pl.BlockSpec((8, 2, block), lambda i, b: (0, 0, i)),
                pl.BlockSpec((2, block), lambda i, b: (0, i)),
                whole,
                whole,
            ]
            + [pl.BlockSpec((rows, block), lambda i, b, j=j: (b[j], i)) for j in range(count)],
            out_specs=pl.BlockSpec((rows * count, d + MASS), lambda i, b: (0, 0)),
        ),
        out_shape=jax.ShapeDtypeStruct((rows * count, d + MASS), F32),
        compiler_params=pltpu.CompilerParams(vmem_limit_bytes=VMEM),
        cost_estimate=pl.CostEstimate(flops=6 * n * d * rows * count, bytes_accessed=4 * n * d, transcendentals=0),
        name="sums",
    )(blocks, stats, own, eh, el, *[p] * count)


def prepare_kernel(c_ref, o_ref):
    c = c_ref[...]
    k = c.shape[0]
    o_ref[:k, :], o_ref[k:, :] = split(c * (SHARPNESS * lax.rsqrt(jnp.sum(c * c, axis=1, keepdims=True) + epsilon)))


def prepare(c):
    return pl.pallas_call(
        prepare_kernel,
        out_shape=jax.ShapeDtypeStruct((2 * c.shape[0], c.shape[1]), BF16),
        compiler_params=pltpu.CompilerParams(vmem_limit_bytes=VMEM),
        name="prepare",
    )(c)


def unit_rms(points):
    return points * lax.rsqrt(jnp.mean(points * points, axis=1, keepdims=True) + epsilon)


def soft_weights(high, low, centers):
    k = centers.shape[0] // 2
    logits = mm(high, centers[:k, :], NT) + mm(high, centers[k:, :], NT) + mm(low, centers[:k, :], NT)
    shifted = jnp.exp(logits - jnp.max(logits, axis=1, keepdims=True))
    return (shifted / jnp.sum(shifted, axis=1, keepdims=True)).T


def store_sums(o_ref, w, high, low):
    wh, wl = split(w)
    d = high.shape[1]
    o_ref[:, :d] = mm(wh, high, NN) + mm(wh, low, NN) + mm(wl, high, NN)
    o_ref[:, d:] = jnp.broadcast_to(jnp.sum(w, axis=1, keepdims=True), (w.shape[0], MASS))


def points_kernel(part_ref, fine_ref, points_ref):
    part = part_ref[0] + part_ref[1] + part_ref[2] + part_ref[3]
    d = fine_ref.shape[1]
    fine = part[:, :d] / part[:, d : d + 1]
    fine_ref[...] = fine
    points_ref[...] = unit_rms(fine)


def points_of(part):
    _, n, d = part.shape
    return pl.pallas_call(
        points_kernel,
        out_shape=[jax.ShapeDtypeStruct((n, d - MASS), F32)] * 2,
        compiler_params=pltpu.CompilerParams(vmem_limit_bytes=VMEM),
        name="points",
    )(part)


def coarse_kernel(slice_ref, own_ref, other_ref, c_ref, o_ref, w_ref):
    high, low = split(jnp.concatenate([own_ref[...], other_ref[...]], axis=0))
    w_ref[...] = soft_weights(high, low, c_ref[...])
    rows = o_ref.shape[0]
    w = w_ref[pl.ds(pl.multiple_of(slice_ref[0] * rows, rows), rows), :]
    store_sums(o_ref, w, high, low)


def coarse_sums(index, own, other, centers, rows):
    n, d = own.shape
    whole = pl.BlockSpec(memory_space=pltpu.VMEM)
    return pl.pallas_call(
        coarse_kernel,
        in_specs=[pl.BlockSpec(memory_space=pltpu.SMEM), whole, whole, whole],
        out_specs=whole,
        out_shape=jax.ShapeDtypeStruct((rows, d + MASS), F32),
        scratch_shapes=[pltpu.VMEM((centers.shape[0] // 2, 2 * n), F32)],
        compiler_params=pltpu.CompilerParams(vmem_limit_bytes=VMEM),
        name="coarse",
    )(index, own, other, centers)


def half_copy(core, ref, coarse_ref, sem):
    rows = ref.shape[0]
    there = pl.ds(pl.multiple_of(core * rows, rows), rows)
    return pltpu.make_async_copy(ref, coarse_ref.at[there, :], sem)


def top_kernel(core_ref, own_ref, c_ref, o_ref, coarse_ref, sem):
    copy = half_copy(core_ref[0], own_ref, coarse_ref, sem)
    copy.start()
    high, low = split(unit_rms(own_ref[...]))
    store_sums(o_ref, soft_weights(high, low, c_ref[...]), high, low)
    copy.wait()


def top_sums(core, own, centers):
    n, d = own.shape
    whole = pl.BlockSpec(memory_space=pltpu.VMEM)
    return pl.pallas_call(
        top_kernel,
        in_specs=[pl.BlockSpec(memory_space=pltpu.SMEM), whole, whole],
        out_specs=[whole, pl.BlockSpec(memory_space=pltpu.HBM)],
        out_shape=[
            jax.ShapeDtypeStruct((centers.shape[0] // 2, d + MASS), F32),
            jax.ShapeDtypeStruct((2 * n, d), F32),
        ],
        scratch_shapes=[pltpu.SemaphoreType.DMA],
        compiler_params=pltpu.CompilerParams(vmem_limit_bytes=VMEM),
        name="top",
    )(core, own, centers)


def final_kernel(core_ref, _, other_ref, part_ref, add_ref, coarse_ref, top_ref, sem):
    copy = half_copy(1 - core_ref[0], other_ref, coarse_ref, sem)
    copy.start()
    part = part_ref[...] + add_ref[...]
    d = top_ref.shape[1]
    top_ref[...] = part[:, :d] / part[:, d : d + 1]
    copy.wait()


def final(core, coarse, other, part, add):
    whole, hbm = pl.BlockSpec(memory_space=pltpu.VMEM), pl.BlockSpec(memory_space=pltpu.HBM)
    return pl.pallas_call(
        final_kernel,
        in_specs=[pl.BlockSpec(memory_space=pltpu.SMEM), hbm, whole, whole, whole],
        out_specs=[hbm, whole],
        out_shape=[
            jax.ShapeDtypeStruct(coarse.shape, F32),
            jax.ShapeDtypeStruct((part.shape[0], coarse.shape[1]), F32),
        ],
        scratch_shapes=[pltpu.SemaphoreType.DMA],
        input_output_aliases={1: 0},
        compiler_params=pltpu.CompilerParams(vmem_limit_bytes=VMEM),
        name="final",
    )(core, coarse, other, part, add)


def spread(value, axes, size):
    return lax.all_to_all(jnp.broadcast_to(value[None], (size, *value.shape)), axes, 0, 0)


def add_up(part, axes, size):
    part = part.reshape(size, part.shape[0] // size, part.shape[1])
    return jnp.sum(lax.all_to_all(part, axes, 0, 0), axis=0)


def swap_core(value):
    return lax.ppermute(value, "c", [(0, 1), (1, 0)])


def shift(value, step):
    return lax.ppermute(value, "x", [(i, (i + step) % 4) for i in range(4)])


def trade(values, axis):
    return [
        lax.ppermute(value, axis, [(i, i ^ flip) for i in range(4)])
        for value, flip in zip(values, (1, 3, 2), strict=True)
    ]


def body(embeddings, centroids, coarse_centroids, top_centroids):
    core = lax.axis_index("c")
    dim = embeddings.shape[1]
    embeddings, centroids = (pltpu.with_memory_space_constraint(a, pltpu.HBM) for a in (embeddings, centroids))
    p, own, eh, el = fit(embeddings, centroids)
    x = lax.axis_index("x")
    mine, theirs = 4 * core, 4 * (1 - core)
    up, down, far = (x + 1) % 4, (x + 3) % 4, (x + 2) % 4
    blocks = [
        jnp.stack(group)
        for group in (
            (theirs + far,),
            (mine + far,),
            (theirs + up, theirs + down, theirs + x),
            (mine + up, mine + down),
            (mine + x,),
        )
    ]
    own, blocks = lax.optimization_barrier((own, blocks))
    stats = spread(own, CENT, 8)
    far_in = swap_core(sums(stats, own, p, eh, el, blocks[0]))
    far_own = sums(stats, own, p, eh, el, blocks[1])
    near_in = swap_core(sums(stats, own, p, eh, el, blocks[2]))
    far_sum = far_own + far_in
    up_part, down_part = shift(far_sum[:32], 1), shift(far_sum[32:], -1)
    blocks[3], _ = lax.optimization_barrier((blocks[3], far_sum))
    near = sums(stats, own, p, eh, el, blocks[3]) + near_in[:128]
    up_sum = jnp.concatenate([near[:32] + up_part, near[32:64]], axis=0)
    down_sum = jnp.concatenate([near[64:96], near[96:] + down_part], axis=0)
    from_down, from_up = shift(up_sum, 1), shift(down_sum, -1)
    blocks[4], _ = lax.optimization_barrier((blocks[4], (up_sum, down_sum)))
    part = sums(stats, own, p, eh, el, blocks[4])
    part = part + near_in[128:] + from_down + from_up
    coarse_centroids, top_centroids, _ = lax.optimization_barrier((coarse_centroids, top_centroids, up_sum))
    coarse_centers, top_centers = prepare(coarse_centroids), prepare(top_centroids)
    part, coarse_centers, top_centers = lax.optimization_barrier((part, coarse_centers, top_centers))
    fine, points = points_of(lax.all_to_all(part.reshape(4, 16, dim + MASS), "zl", 0, 0))

    points = jnp.concatenate([points, *trade([points] * 3, "x")], axis=0)
    part = coarse_sums((core * 4 + x).reshape(1), points, swap_core(points), coarse_centers, 64)
    part = add_up(part, ("y", "zh", "zl"), 32)
    coarse = part[:, :dim] / part[:, dim : dim + 1]
    coarse = spread(coarse, ("zh", "zl"), 8).reshape(16, dim)
    coarse = spread(coarse, ("x", "y"), 16).reshape(256, dim)
    other = swap_core(coarse)
    part, new_coarse = top_sums(core.reshape(1), coarse, top_centers)
    new_coarse, new_top = final(core.reshape(1), new_coarse, other, part, swap_core(part))
    return (fine[None], new_coarse, new_top)


def solution(mesh):
    fold = Mesh(mesh.devices.reshape(4, 4, 2, 2, 4), DP + CENT)
    in_specs = (P(DP, None), P(CENT, None), P(), P())
    out_specs = (P(CENT, DP, None), P(), P())
    return jax.shard_map(body, mesh=fold, in_specs=in_specs, out_specs=out_specs, check_vma=False)
```

```python
import functools

import jax
import jax.numpy as jnp
from jax import lax
from jax.experimental import pallas as pl
from jax.experimental.pallas import tpu as pltpu
from jax.sharding import Mesh, PartitionSpec as P

epsilon = 1e-06
SHARPNESS = 1.5
DP = ("x", "zl", "c")
CENT = ("zh", "y")
MASS = 128
F32, BF16 = jnp.float32, jnp.bfloat16
VMEM = 36 * 2**20
NT = (((1,), (1,)), ((), ()))
NN = (((1,), (0,)), ((), ()))


def split(value):
    high = value.astype(BF16)
    return high, (value - high.astype(F32)).astype(BF16)


def mm(left, right, dims):
    return lax.dot_general(left, right, dims, preferred_element_type=F32)


def fit_kernel(step, e_hbm, c_hbm, p_ref, stat_ref, eh_ref, el_ref, chl, c_ref, e_ref, sems):
    (n, _), k = e_ref.shape, c_ref.shape[0]
    pieces = 4
    copies = []
    for i in range(pieces):
        rows = pl.ds(i * (k // pieces), k // pieces)
        copies.append(pltpu.make_async_copy(c_hbm.at[rows, :], c_ref.at[rows, :], sems.at[n // step + i]))
    for i in range(n // step):
        rows = pl.ds(i * step, step)
        copies.append(pltpu.make_async_copy(e_hbm.at[rows, :], e_ref.at[rows, :], sems.at[i]))
    for copy in copies:
        copy.start()
    for chip in range(16):
        if chip % (16 // pieces) == 0:
            copies[chip // (16 // pieces)].wait()
        for core in range(2):
            here, there = (chip * 2 + core) * 16, (core * 16 + chip) * 16
            c = c_ref[here : here + 16, :]
            c = c * (SHARPNESS * lax.rsqrt(jnp.sum(c * c, axis=1, keepdims=True) + epsilon))
            chl[there : there + 16, :], chl[k + there : k + there + 16, :] = split(c)

    @pl.loop(0, n // step)
    def _(i):
        rows = pl.ds(pl.multiple_of(i * step, step), step)
        pltpu.make_async_copy(e_hbm.at[rows, :], e_ref.at[rows, :], sems.at[i]).wait()
        eh, el = split(e_ref[rows, :])
        eh_ref[rows, :] = eh
        el_ref[rows, :] = el
        both = mm(chl[...], eh, NT)
        logits = both[:k] + both[k:] + mm(chl[:k, :], el, NT)
        top = jnp.max(logits, axis=0, keepdims=True)
        p = jnp.exp(logits - top)
        p_ref[:, rows] = p
        stat_ref[0:1, rows] = top
        stat_ref[1:2, rows] = jnp.sum(p, axis=0, keepdims=True)


def fit(e, c, step=512):
    (n, d), k = e.shape, c.shape[0]
    return pl.pallas_call(
        functools.partial(fit_kernel, step),
        in_specs=[pl.BlockSpec(memory_space=pltpu.HBM)] * 2,
        out_specs=[pl.BlockSpec(memory_space=pltpu.VMEM)] * 4,
        out_shape=[
            jax.ShapeDtypeStruct((k, n), F32),
            jax.ShapeDtypeStruct((2, n), F32),
            jax.ShapeDtypeStruct((n, d), BF16),
            jax.ShapeDtypeStruct((n, d), BF16),
        ],
        scratch_shapes=[
            pltpu.VMEM((2 * k, d), BF16),
            pltpu.VMEM((k, d), F32),
            pltpu.VMEM((n, d), F32),
            pltpu.SemaphoreType.DMA((n // step + 4,)),
        ],
        compiler_params=pltpu.CompilerParams(vmem_limit_bytes=VMEM),
        name="fit",
    )(e, c)


def sums_kernel(_, stats_ref, own_ref, eh_ref, el_ref, *refs):
    *p_refs, o_ref = refs

    @pl.when(pl.program_id(0) == 0)
    def _():
        o_ref[...] = jnp.zeros_like(o_ref)

    tops, totals = stats_ref[:, 0, :], stats_ref[:, 1, :]
    top = jnp.max(tops, axis=0, keepdims=True)
    total = jnp.sum(totals * jnp.exp(tops - top), axis=0, keepdims=True)
    scale = jnp.exp(own_ref[0:1, :] - top) / total
    w = jnp.concatenate([p_ref[...] for p_ref in p_refs], axis=0) * scale
    (k, block), d = w.shape, eh_ref.shape[1]
    here = pl.ds(pl.multiple_of(pl.program_id(0) * block, block), block)
    wh, wl = split(w)
    both = mm(jnp.concatenate([wh, wl], axis=0), eh_ref[here, :], NN)
    part = both[:k] + both[k:] + mm(wh, el_ref[here, :], NN)
    mass = jnp.sum(w, axis=1, keepdims=True)
    lane = lax.broadcasted_iota(jnp.int32, (8, 128), 1)
    tile = 0
    for row in range(0, k, 16):
        for first in (row, row + 8):
            for column in range(0, d, 128):
                o_ref[tile] += part[first : first + 8, column : column + 128]
                tile += 1
        o_ref[tile] += jnp.where(lane == 0, mass[row : row + 8], mass[row + 8 : row + 16])
        tile += 1


def sums(stats, own, p, eh, el, blocks, rows=64, block=1024):
    n, d = eh.shape
    count = blocks.shape[0]
    tiles = rows * count // 16 * (2 * d // 128 + 1)
    whole = pl.BlockSpec(memory_space=pltpu.VMEM)
    return pl.pallas_call(
        sums_kernel,
        grid_spec=pltpu.PrefetchScalarGridSpec(
            num_scalar_prefetch=1,
            grid=(n // block,),
            in_specs=[
                pl.BlockSpec((8, 2, block), lambda i, b: (0, 0, i)),
                pl.BlockSpec((2, block), lambda i, b: (0, i)),
                whole,
                whole,
            ]
            + [pl.BlockSpec((rows, block), lambda i, b, j=j: (b[j], i)) for j in range(count)],
            out_specs=pl.BlockSpec((tiles, 8, 128), lambda i, b: (0, 0, 0)),
        ),
        out_shape=jax.ShapeDtypeStruct((tiles, 8, 128), F32),
        compiler_params=pltpu.CompilerParams(vmem_limit_bytes=VMEM),
        cost_estimate=pl.CostEstimate(flops=6 * n * d * rows * count, bytes_accessed=4 * n * d, transcendentals=0),
        name="sums",
    )(blocks, stats, own, eh, el, *[p] * count)


def prepare_kernel(c_ref, o_ref):
    c = c_ref[...]
    k = c.shape[0]
    o_ref[:k, :], o_ref[k:, :] = split(c * (SHARPNESS * lax.rsqrt(jnp.sum(c * c, axis=1, keepdims=True) + epsilon)))


def prepare(c):
    return pl.pallas_call(
        prepare_kernel,
        out_shape=jax.ShapeDtypeStruct((2 * c.shape[0], c.shape[1]), BF16),
        compiler_params=pltpu.CompilerParams(vmem_limit_bytes=VMEM),
        name="prepare",
    )(c)


def unit_rms(points):
    return points * lax.rsqrt(jnp.mean(points * points, axis=1, keepdims=True) + epsilon)


def soft_weights(high, low, centers):
    k = centers.shape[0] // 2
    logits = mm(high, centers[:k, :], NT) + mm(high, centers[k:, :], NT) + mm(low, centers[:k, :], NT)
    shifted = jnp.exp(logits - jnp.max(logits, axis=1, keepdims=True))
    return (shifted / jnp.sum(shifted, axis=1, keepdims=True)).T


def store_sums(o_ref, w, high, low):
    wh, wl = split(w)
    d = high.shape[1]
    o_ref[:, :d] = mm(wh, high, NN) + mm(wh, low, NN) + mm(wl, high, NN)
    o_ref[:, d:] = jnp.broadcast_to(jnp.sum(w, axis=1, keepdims=True), (w.shape[0], MASS))


def points_kernel(part_ref, fine_ref, points_ref):
    d = fine_ref.shape[1]
    mass = sum(part_ref[i, 2 * d // 128] for i in range(4))
    for half in range(2):
        first = half * (d // 128)
        tiles = [sum(part_ref[i, first + j] for i in range(4)) for j in range(d // 128)]
        fine = jnp.concatenate(tiles, axis=1) / mass[:, half : half + 1]
        fine_ref[half * 8 : half * 8 + 8, :] = fine
        points_ref[half * 8 : half * 8 + 8, :] = unit_rms(fine)


def points_of(part, d):
    return pl.pallas_call(
        points_kernel,
        out_shape=[jax.ShapeDtypeStruct((16, d), F32)] * 2,
        compiler_params=pltpu.CompilerParams(vmem_limit_bytes=VMEM),
        name="points",
    )(part)


def coarse_kernel(slice_ref, own_ref, other_ref, c_ref, o_ref, w_ref):
    high, low = split(jnp.concatenate([own_ref[...], other_ref[...]], axis=0))
    w_ref[...] = soft_weights(high, low, c_ref[...])
    rows = o_ref.shape[0]
    w = w_ref[pl.ds(pl.multiple_of(slice_ref[0] * rows, rows), rows), :]
    store_sums(o_ref, w, high, low)


def coarse_sums(index, own, other, centers, rows):
    n, d = own.shape
    whole = pl.BlockSpec(memory_space=pltpu.VMEM)
    return pl.pallas_call(
        coarse_kernel,
        in_specs=[pl.BlockSpec(memory_space=pltpu.SMEM), whole, whole, whole],
        out_specs=whole,
        out_shape=jax.ShapeDtypeStruct((rows, d + MASS), F32),
        scratch_shapes=[pltpu.VMEM((centers.shape[0] // 2, 2 * n), F32)],
        compiler_params=pltpu.CompilerParams(vmem_limit_bytes=VMEM),
        name="coarse",
    )(index, own, other, centers)


def half_copy(core, ref, coarse_ref, sem):
    rows = ref.shape[0]
    there = pl.ds(pl.multiple_of(core * rows, rows), rows)
    return pltpu.make_async_copy(ref, coarse_ref.at[there, :], sem)


def top_kernel(core_ref, own_ref, c_ref, o_ref, coarse_ref, sem):
    copy = half_copy(core_ref[0], own_ref, coarse_ref, sem)
    copy.start()
    high, low = split(unit_rms(own_ref[...]))
    store_sums(o_ref, soft_weights(high, low, c_ref[...]), high, low)
    copy.wait()


def top_sums(core, own, centers):
    n, d = own.shape
    whole = pl.BlockSpec(memory_space=pltpu.VMEM)
    return pl.pallas_call(
        top_kernel,
        in_specs=[pl.BlockSpec(memory_space=pltpu.SMEM), whole, whole],
        out_specs=[whole, pl.BlockSpec(memory_space=pltpu.HBM)],
        out_shape=[
            jax.ShapeDtypeStruct((centers.shape[0] // 2, d + MASS), F32),
            jax.ShapeDtypeStruct((2 * n, d), F32),
        ],
        scratch_shapes=[pltpu.SemaphoreType.DMA],
        compiler_params=pltpu.CompilerParams(vmem_limit_bytes=VMEM),
        name="top",
    )(core, own, centers)


def final_kernel(core_ref, _, other_ref, part_ref, add_ref, coarse_ref, top_ref, sem):
    copy = half_copy(1 - core_ref[0], other_ref, coarse_ref, sem)
    copy.start()
    part = part_ref[...] + add_ref[...]
    d = top_ref.shape[1]
    top_ref[...] = part[:, :d] / part[:, d : d + 1]
    copy.wait()


def final(core, coarse, other, part, add):
    whole, hbm = pl.BlockSpec(memory_space=pltpu.VMEM), pl.BlockSpec(memory_space=pltpu.HBM)
    return pl.pallas_call(
        final_kernel,
        in_specs=[pl.BlockSpec(memory_space=pltpu.SMEM), hbm, whole, whole, whole],
        out_specs=[hbm, whole],
        out_shape=[
            jax.ShapeDtypeStruct(coarse.shape, F32),
            jax.ShapeDtypeStruct((part.shape[0], coarse.shape[1]), F32),
        ],
        scratch_shapes=[pltpu.SemaphoreType.DMA],
        input_output_aliases={1: 0},
        compiler_params=pltpu.CompilerParams(vmem_limit_bytes=VMEM),
        name="final",
    )(core, coarse, other, part, add)


def spread(value, axes, size):
    return lax.all_to_all(jnp.broadcast_to(value[None], (size, *value.shape)), axes, 0, 0)


def add_up(part, axes, size):
    part = part.reshape(size, part.shape[0] // size, part.shape[1])
    return jnp.sum(lax.all_to_all(part, axes, 0, 0), axis=0)


def swap_core(value):
    return lax.ppermute(value, "c", [(0, 1), (1, 0)])


def shift(value, step):
    return lax.ppermute(value, "x", [(i, (i + step) % 4) for i in range(4)])


def trade(values, axis):
    return [
        lax.ppermute(value, axis, [(i, i ^ flip) for i in range(4)])
        for value, flip in zip(values, (1, 3, 2), strict=True)
    ]


def body(embeddings, centroids, coarse_centroids, top_centroids):
    core = lax.axis_index("c")
    dim = embeddings.shape[1]
    embeddings, centroids = (pltpu.with_memory_space_constraint(a, pltpu.HBM) for a in (embeddings, centroids))
    p, own, eh, el = fit(embeddings, centroids)
    x = lax.axis_index("x")
    mine, theirs = 4 * core, 4 * (1 - core)
    up, down, far = (x + 1) % 4, (x + 3) % 4, (x + 2) % 4
    blocks = [
        jnp.stack(group)
        for group in (
            (theirs + far,),
            (mine + far,),
            (theirs + up, theirs + down, theirs + x),
            (mine + up, mine + down),
            (mine + x,),
        )
    ]
    own, blocks = lax.optimization_barrier((own, blocks))
    stats = spread(own, CENT, 8)
    far_in = swap_core(sums(stats, own, p, eh, el, blocks[0]))
    far_own = sums(stats, own, p, eh, el, blocks[1])
    near_in = swap_core(sums(stats, own, p, eh, el, blocks[2]))
    far_sum = far_own + far_in
    up_part, down_part = shift(far_sum[:34], 1), shift(far_sum[34:], -1)
    blocks[3], _ = lax.optimization_barrier((blocks[3], far_sum))
    near = sums(stats, own, p, eh, el, blocks[3]) + near_in[:136]
    up_sum = jnp.concatenate([near[:34] + up_part, near[34:68]], axis=0)
    down_sum = jnp.concatenate([near[68:102], near[102:] + down_part], axis=0)
    from_down, from_up = shift(up_sum, 1), shift(down_sum, -1)
    blocks[4], _ = lax.optimization_barrier((blocks[4], (up_sum, down_sum)))
    part = sums(stats, own, p, eh, el, blocks[4])
    part = part + near_in[136:] + from_down + from_up
    coarse_centroids, top_centroids, _ = lax.optimization_barrier((coarse_centroids, top_centroids, up_sum))
    coarse_centers, top_centers = prepare(coarse_centroids), prepare(top_centroids)
    part, coarse_centers, top_centers = lax.optimization_barrier((part, coarse_centers, top_centers))
    fine, points = points_of(lax.all_to_all(part.reshape(4, 17, 8, 128), "zl", 0, 0), dim)

    points = jnp.concatenate([points, *trade([points] * 3, "x")], axis=0)
    part = coarse_sums((core * 4 + x).reshape(1), points, swap_core(points), coarse_centers, 64)
    part = add_up(part, ("y", "zh", "zl"), 32)
    coarse = part[:, :dim] / part[:, dim : dim + 1]
    coarse = spread(coarse, ("zh", "zl"), 8).reshape(16, dim)
    coarse = spread(coarse, ("x", "y"), 16).reshape(256, dim)
    other = swap_core(coarse)
    part, new_coarse = top_sums(core.reshape(1), coarse, top_centers)
    new_coarse, new_top = final(core.reshape(1), new_coarse, other, part, swap_core(part))
    return (fine[None], new_coarse, new_top)


def solution(mesh):
    fold = Mesh(mesh.devices.reshape(4, 4, 2, 2, 4), DP + CENT)
    in_specs = (P(DP, None), P(CENT, None), P(), P())
    out_specs = (P(CENT, DP, None), P(), P())
    return jax.shard_map(body, mesh=fold, in_specs=in_specs, out_specs=out_specs, check_vma=False)
```

```python
import functools

import jax
import jax.numpy as jnp
from jax import lax
from jax.experimental import pallas as pl
from jax.experimental.pallas import tpu as pltpu
from jax.sharding import Mesh, PartitionSpec as P

epsilon = 1e-06
SHARPNESS = 1.5
DP = ("x", "zl", "c")
CENT = ("zh", "y")
MASS = 128
F32, BF16 = jnp.float32, jnp.bfloat16
VMEM = 36 * 2**20
NT = (((1,), (1,)), ((), ()))
NN = (((1,), (0,)), ((), ()))


def split(value):
    high = value.astype(BF16)
    return high, (value - high.astype(F32)).astype(BF16)


def mm(left, right, dims):
    return lax.dot_general(left, right, dims, preferred_element_type=F32)


def fit_kernel(step, e_hbm, c_hbm, p_ref, stat_ref, eh_ref, el_ref, chl, c_ref, e_ref, sems):
    (n, _), k = e_ref.shape, c_ref.shape[0]
    pieces = 4
    copies = []
    for i in range(pieces):
        rows = pl.ds(i * (k // pieces), k // pieces)
        copies.append(pltpu.make_async_copy(c_hbm.at[rows, :], c_ref.at[rows, :], sems.at[n // step + i]))
    for i in range(n // step):
        rows = pl.ds(i * step, step)
        copies.append(pltpu.make_async_copy(e_hbm.at[rows, :], e_ref.at[rows, :], sems.at[i]))
    for copy in copies:
        copy.start()
    for chip in range(16):
        if chip % (16 // pieces) == 0:
            copies[chip // (16 // pieces)].wait()
        for core in range(2):
            here, there = (chip * 2 + core) * 16, (core * 16 + chip) * 16
            c = c_ref[here : here + 16, :]
            c = c * (SHARPNESS * lax.rsqrt(jnp.sum(c * c, axis=1, keepdims=True) + epsilon))
            chl[there : there + 16, :], chl[k + there : k + there + 16, :] = split(c)

    @pl.loop(0, n // step)
    def _(i):
        rows = pl.ds(pl.multiple_of(i * step, step), step)
        pltpu.make_async_copy(e_hbm.at[rows, :], e_ref.at[rows, :], sems.at[i]).wait()
        eh, el = split(e_ref[rows, :])
        eh_ref[rows, :] = eh
        el_ref[rows, :] = el
        both = mm(chl[...], eh, NT)
        logits = both[:k] + both[k:] + mm(chl[:k, :], el, NT)
        top = jnp.max(logits, axis=0, keepdims=True)
        p = jnp.exp(logits - top)
        p_ref[:, rows] = p
        stat_ref[0:1, rows] = top
        stat_ref[1:2, rows] = jnp.sum(p, axis=0, keepdims=True)


def fit(e, c, step=512):
    (n, d), k = e.shape, c.shape[0]
    return pl.pallas_call(
        functools.partial(fit_kernel, step),
        in_specs=[pl.BlockSpec(memory_space=pltpu.HBM)] * 2,
        out_specs=[pl.BlockSpec(memory_space=pltpu.VMEM)] * 4,
        out_shape=[
            jax.ShapeDtypeStruct((k, n), F32),
            jax.ShapeDtypeStruct((2, n), F32),
            jax.ShapeDtypeStruct((n, d), BF16),
            jax.ShapeDtypeStruct((n, d), BF16),
        ],
        scratch_shapes=[
            pltpu.VMEM((2 * k, d), BF16),
            pltpu.VMEM((k, d), F32),
            pltpu.VMEM((n, d), F32),
            pltpu.SemaphoreType.DMA((n // step + 4,)),
        ],
        compiler_params=pltpu.CompilerParams(vmem_limit_bytes=VMEM),
        name="fit",
    )(e, c)


def sums_kernel(_, stats_ref, own_ref, eh_ref, el_ref, *refs):
    *p_refs, o_ref = refs

    @pl.when(pl.program_id(0) == 0)
    def _():
        o_ref[...] = jnp.zeros_like(o_ref)

    tops, totals = stats_ref[:, 0, :], stats_ref[:, 1, :]
    top = jnp.max(tops, axis=0, keepdims=True)
    total = jnp.sum(totals * jnp.exp(tops - top), axis=0, keepdims=True)
    scale = jnp.exp(own_ref[0:1, :] - top) / total
    w = jnp.concatenate([p_ref[...] for p_ref in p_refs], axis=0) * scale
    (k, block), d = w.shape, eh_ref.shape[1]
    here = pl.ds(pl.multiple_of(pl.program_id(0) * block, block), block)
    wh, wl = split(w)
    both = mm(jnp.concatenate([wh, wl], axis=0), eh_ref[here, :], NN)
    part = both[:k] + both[k:] + mm(wh, el_ref[here, :], NN)
    mass = jnp.sum(w, axis=1, keepdims=True)
    lane = lax.broadcasted_iota(jnp.int32, (8, 128), 1)
    tile = 0
    for row in range(0, k, 16):
        for first in (row, row + 8):
            for column in range(0, d, 128):
                o_ref[tile] += part[first : first + 8, column : column + 128]
                tile += 1
        o_ref[tile] += jnp.where(lane == 0, mass[row : row + 8], mass[row + 8 : row + 16])
        tile += 1


def sums(stats, own, p, eh, el, blocks, rows=64, block=1024):
    n, d = eh.shape
    count = blocks.shape[0]
    tiles = rows * count // 16 * (2 * d // 128 + 1)
    whole = pl.BlockSpec(memory_space=pltpu.VMEM)
    return pl.pallas_call(
        sums_kernel,
        grid_spec=pltpu.PrefetchScalarGridSpec(
            num_scalar_prefetch=1,
            grid=(n // block,),
            in_specs=[
                pl.BlockSpec((8, 2, block), lambda i, b: (0, 0, i)),
                pl.BlockSpec((2, block), lambda i, b: (0, i)),
                whole,
                whole,
            ]
            + [pl.BlockSpec((rows, block), lambda i, b, j=j: (b[j], i)) for j in range(count)],
            out_specs=pl.BlockSpec((tiles, 8, 128), lambda i, b: (0, 0, 0)),
        ),
        out_shape=jax.ShapeDtypeStruct((tiles, 8, 128), F32),
        compiler_params=pltpu.CompilerParams(vmem_limit_bytes=VMEM),
        cost_estimate=pl.CostEstimate(flops=6 * n * d * rows * count, bytes_accessed=4 * n * d, transcendentals=0),
        name="sums",
    )(blocks, stats, own, eh, el, *[p] * count)


def prepare_kernel(c_ref, o_ref):
    c = c_ref[...]
    k = c.shape[0]
    o_ref[:k, :], o_ref[k:, :] = split(c * (SHARPNESS * lax.rsqrt(jnp.sum(c * c, axis=1, keepdims=True) + epsilon)))


def prepare(c):
    return pl.pallas_call(
        prepare_kernel,
        out_shape=jax.ShapeDtypeStruct((2 * c.shape[0], c.shape[1]), BF16),
        compiler_params=pltpu.CompilerParams(vmem_limit_bytes=VMEM),
        name="prepare",
    )(c)


def unit_rms(points):
    return points * lax.rsqrt(jnp.mean(points * points, axis=1, keepdims=True) + epsilon)


def soft_weights(high, low, centers):
    k = centers.shape[0] // 2
    logits = mm(high, centers[:k, :], NT) + mm(high, centers[k:, :], NT) + mm(low, centers[:k, :], NT)
    shifted = jnp.exp(logits - jnp.max(logits, axis=1, keepdims=True))
    return (shifted / jnp.sum(shifted, axis=1, keepdims=True)).T


def store_sums(o_ref, w, high, low):
    wh, wl = split(w)
    d = high.shape[1]
    o_ref[:, :d] = mm(wh, high, NN) + mm(wh, low, NN) + mm(wl, high, NN)
    o_ref[:, d:] = jnp.broadcast_to(jnp.sum(w, axis=1, keepdims=True), (w.shape[0], MASS))


def points_kernel(part_ref, fine_ref, points_ref):
    d = fine_ref.shape[1]
    mass = sum(part_ref[i, 2 * d // 128] for i in range(4))
    for half in range(2):
        first = half * (d // 128)
        tiles = [sum(part_ref[i, first + j] for i in range(4)) for j in range(d // 128)]
        fine = jnp.concatenate(tiles, axis=1) / mass[:, half : half + 1]
        fine_ref[half * 8 : half * 8 + 8, :] = fine
        points_ref[half * 8 : half * 8 + 8, :] = unit_rms(fine)


def points_of(part, d):
    return pl.pallas_call(
        points_kernel,
        out_shape=[jax.ShapeDtypeStruct((16, d), F32)] * 2,
        compiler_params=pltpu.CompilerParams(vmem_limit_bytes=VMEM),
        name="points",
    )(part)


def coarse_kernel(slice_ref, own_ref, other_ref, c_ref, o_ref, w_ref):
    high, low = split(jnp.concatenate([own_ref[...], other_ref[...]], axis=0))
    w_ref[...] = soft_weights(high, low, c_ref[...])
    rows = o_ref.shape[0]
    w = w_ref[pl.ds(pl.multiple_of(slice_ref[0] * rows, rows), rows), :]
    store_sums(o_ref, w, high, low)


def coarse_sums(index, own, other, centers, rows):
    n, d = own.shape
    whole = pl.BlockSpec(memory_space=pltpu.VMEM)
    return pl.pallas_call(
        coarse_kernel,
        in_specs=[pl.BlockSpec(memory_space=pltpu.SMEM), whole, whole, whole],
        out_specs=whole,
        out_shape=jax.ShapeDtypeStruct((rows, d + MASS), F32),
        scratch_shapes=[pltpu.VMEM((centers.shape[0] // 2, 2 * n), F32)],
        compiler_params=pltpu.CompilerParams(vmem_limit_bytes=VMEM),
        name="coarse",
    )(index, own, other, centers)


def half_copy(core, ref, coarse_ref, sem):
    rows = ref.shape[0]
    there = pl.ds(pl.multiple_of(core * rows, rows), rows)
    return pltpu.make_async_copy(ref, coarse_ref.at[there, :], sem)


def top_kernel(core_ref, own_ref, c_ref, o_ref, coarse_ref, sem):
    copy = half_copy(core_ref[0], own_ref, coarse_ref, sem)
    copy.start()
    high, low = split(unit_rms(own_ref[...]))
    store_sums(o_ref, soft_weights(high, low, c_ref[...]), high, low)
    copy.wait()


def top_sums(core, own, centers):
    n, d = own.shape
    whole = pl.BlockSpec(memory_space=pltpu.VMEM)
    return pl.pallas_call(
        top_kernel,
        in_specs=[pl.BlockSpec(memory_space=pltpu.SMEM), whole, whole],
        out_specs=[whole, pl.BlockSpec(memory_space=pltpu.HBM)],
        out_shape=[
            jax.ShapeDtypeStruct((centers.shape[0] // 2, d + MASS), F32),
            jax.ShapeDtypeStruct((2 * n, d), F32),
        ],
        scratch_shapes=[pltpu.SemaphoreType.DMA],
        compiler_params=pltpu.CompilerParams(vmem_limit_bytes=VMEM),
        name="top",
    )(core, own, centers)


def final_kernel(core_ref, _, other_ref, part_ref, add_ref, coarse_ref, top_ref, sem):
    copy = half_copy(1 - core_ref[0], other_ref, coarse_ref, sem)
    copy.start()
    part = part_ref[...] + add_ref[...]
    d = top_ref.shape[1]
    top_ref[...] = part[:, :d] / part[:, d : d + 1]
    copy.wait()


def final(core, coarse, other, part, add):
    whole, hbm = pl.BlockSpec(memory_space=pltpu.VMEM), pl.BlockSpec(memory_space=pltpu.HBM)
    return pl.pallas_call(
        final_kernel,
        in_specs=[pl.BlockSpec(memory_space=pltpu.SMEM), hbm, whole, whole, whole],
        out_specs=[hbm, whole],
        out_shape=[
            jax.ShapeDtypeStruct(coarse.shape, F32),
            jax.ShapeDtypeStruct((part.shape[0], coarse.shape[1]), F32),
        ],
        scratch_shapes=[pltpu.SemaphoreType.DMA],
        input_output_aliases={1: 0},
        compiler_params=pltpu.CompilerParams(vmem_limit_bytes=VMEM),
        name="final",
    )(core, coarse, other, part, add)


def spread(value, axes, size):
    return lax.all_to_all(jnp.broadcast_to(value[None], (size, *value.shape)), axes, 0, 0)


def add_up(part, axes, size):
    part = part.reshape(size, part.shape[0] // size, part.shape[1])
    return jnp.sum(lax.all_to_all(part, axes, 0, 0), axis=0)


def swap_core(value):
    return lax.ppermute(value, "c", [(0, 1), (1, 0)])


def shift(value, step):
    return lax.ppermute(value, "x", [(i, (i + step) % 4) for i in range(4)])


def trade(values, axis):
    return [
        lax.ppermute(value, axis, [(i, i ^ flip) for i in range(4)])
        for value, flip in zip(values, (1, 3, 2), strict=True)
    ]


def body(embeddings, centroids, coarse_centroids, top_centroids):
    core = lax.axis_index("c")
    dim = embeddings.shape[1]
    embeddings, centroids = (pltpu.with_memory_space_constraint(a, pltpu.HBM) for a in (embeddings, centroids))
    p, own, eh, el = fit(embeddings, centroids)
    x = lax.axis_index("x")
    mine, theirs = 4 * core, 4 * (1 - core)
    up, down, far = (x + 1) % 4, (x + 3) % 4, (x + 2) % 4
    blocks = [
        jnp.stack(group)
        for group in (
            (theirs + far, mine + far),
            (theirs + up, theirs + down, theirs + x),
            (mine + up, mine + down),
            (mine + x,),
        )
    ]
    own, blocks = lax.optimization_barrier((own, blocks))
    stats = spread(own, CENT, 8)
    both = sums(stats, own, p, eh, el, blocks[0])
    far_in, far_own = swap_core(both[:68]), both[68:]
    blocks[1], _ = lax.optimization_barrier((blocks[1], both))
    near_in = swap_core(sums(stats, own, p, eh, el, blocks[1]))
    far_sum = far_own + far_in
    up_part, down_part = shift(far_sum[:34], 1), shift(far_sum[34:], -1)
    blocks[2], _ = lax.optimization_barrier((blocks[2], far_sum))
    near = sums(stats, own, p, eh, el, blocks[2]) + near_in[:136]
    up_sum = jnp.concatenate([near[:34] + up_part, near[34:68]], axis=0)
    down_sum = jnp.concatenate([near[68:102], near[102:] + down_part], axis=0)
    from_down, from_up = shift(up_sum, 1), shift(down_sum, -1)
    blocks[3], _ = lax.optimization_barrier((blocks[3], (up_sum, down_sum)))
    part = sums(stats, own, p, eh, el, blocks[3])
    part = part + near_in[136:] + from_down + from_up
    coarse_centroids, top_centroids, _ = lax.optimization_barrier((coarse_centroids, top_centroids, up_sum))
    coarse_centers, top_centers = prepare(coarse_centroids), prepare(top_centroids)
    part, coarse_centers, top_centers = lax.optimization_barrier((part, coarse_centers, top_centers))
    fine, points = points_of(lax.all_to_all(part.reshape(4, 17, 8, 128), "zl", 0, 0), dim)

    points = jnp.concatenate([points, *trade([points] * 3, "x")], axis=0)
    part = coarse_sums((core * 4 + x).reshape(1), points, swap_core(points), coarse_centers, 64)
    part = add_up(part, ("y", "zh", "zl"), 32)
    coarse = part[:, :dim] / part[:, dim : dim + 1]
    coarse = spread(coarse, ("zh", "zl"), 8).reshape(16, dim)
    coarse = spread(coarse, ("x", "y"), 16).reshape(256, dim)
    other = swap_core(coarse)
    part, new_coarse = top_sums(core.reshape(1), coarse, top_centers)
    new_coarse, new_top = final(core.reshape(1), new_coarse, other, part, swap_core(part))
    return (fine[None], new_coarse, new_top)


def solution(mesh):
    fold = Mesh(mesh.devices.reshape(4, 4, 2, 2, 4), DP + CENT)
    in_specs = (P(DP, None), P(CENT, None), P(), P())
    out_specs = (P(CENT, DP, None), P(), P())
    return jax.shard_map(body, mesh=fold, in_specs=in_specs, out_specs=out_specs, check_vma=False)
```
